32 devices in a mesh: gx: 4 (over y, core), gy: 4 (over z), gz: 2 (over x).
Axes of the slice: x: 2, y: 2, z: 4, core: 2. Of those that a mesh axis runs over, the one named last changes fastest.
Arguments:
- tokens: bfloat16 [1024, 8192], P(('gx', 'gy'), 'gz'), may hold values from -6 to 6
- gate_weight: bfloat16 [8192, 28672], P('gz', ('gx', 'gy')), may hold values from -0.0625 to 0.0625
- up_weight: bfloat16 [8192, 28672], P('gz', ('gx', 'gy')), may hold values from -0.0625 to 0.0625
- down_weight: bfloat16 [28672, 8192], P(('gx', 'gy'), 'gz'), may hold values from -0.03125 to 0.03125
Outputs:
- layer_output: bfloat16 [1024, 8192], P(('gx', 'gy'), 'gz')
The draws below stay inside these ranges and needn't reach their ends.
All inputs are finite; a program needn't handle non-finite values.
Results may differ from the reference program's by a relative error of at most 0.029.
Values may be sent and summed in bfloat16 or wider, within the bound.
No kernel may reach another device: no remote copies, remote signals or barrier semaphores. Data moves between devices by JAX's collectives and lax.ppermute only.
A program may use at most 256 MiB of HBM per device.

```python
import jax
import jax.numpy as jnp
from jax import lax

D = 8192
FF = 28672
TOKENS = 1024
N_GZ = 2


def steps_of(rng, extent, split, least, high):
    level = 1.0
    for dim, shards_of in split:
        heights = jax.random.uniform(jax.random.fold_in(jax.random.fold_in(rng, 6), dim), (shards_of,), jnp.float32, least / len(split), high / len(split))
        level = level * jnp.repeat(jnp.exp(heights), extent[dim] // shards_of).reshape((-1,) + (1,) * (len(extent) - 1 - dim))
    return level


def noise(own_key, shape, scale, most, shards=(), dtype=jnp.bfloat16):
    factor_of = steps_of(own_key, shape, shards, -0.22, 0.18) if shards else 1.0
    result = jax.random.normal(own_key, shape, jnp.float32) * scale * factor_of
    return jnp.minimum(jnp.maximum(result, -most), most).astype(dtype)


def setup_inputs(seed: int = 0) -> dict:
    seeds = jax.random.split(jax.random.key(seed), 5)
    tokens = noise(seeds[0], (TOKENS, D), 1.0, 6.0, ((0, 16), (1, 2)))
    gate_weight = noise(seeds[1], (D, FF), D ** -0.5, 0.0625, ((0, 2), (1, 16)))
    up_weight = noise(seeds[2], (D, FF), D ** -0.5, 0.0625, ((0, 2), (1, 16)))
    down_weight = noise(seeds[3], (FF, D), FF ** -0.5, 0.03125, ((0, 16), (1, 2)))
    return dict(tokens=tokens, gate_weight=gate_weight, up_weight=up_weight, down_weight=down_weight)


def blocked_sum(tokens, weight_matrix):
    span_width = D // N_GZ
    running = jnp.zeros((tokens.shape[0], weight_matrix.shape[1]), jnp.float32)
    for segment in range(N_GZ):
        left_part = tokens[:, segment * span_width:(segment + 1) * span_width]
        right_part = weight_matrix[segment * span_width:(segment + 1) * span_width, :]
        product = jnp.dot(left_part, right_part, preferred_element_type=jnp.float32)
        rounded = lax.optimization_barrier(product.astype(jnp.bfloat16))
        running = running + rounded.astype(jnp.float32)
    return running


def reference(tokens, gate_weight, up_weight, down_weight):
    gate = blocked_sum(tokens, gate_weight)
    up_sum = blocked_sum(tokens, up_weight)
    hidden = (jax.nn.silu(gate) * up_sum).astype(jnp.bfloat16)
    return jnp.dot(hidden, down_weight, preferred_element_type=jnp.float32).astype(jnp.bfloat16)
```

```python
import functools

import jax
import jax.numpy as jnp
from jax import lax
from jax.experimental import pallas as pl
from jax.experimental.pallas import tpu as pltpu
from jax.sharding import PartitionSpec as P

BF16 = jnp.bfloat16
F32 = jnp.float32
MIB = 1 << 20


def tile_of(width, most):
    return max(t for t in range(128, most + 1, 128) if width % t == 0)


def in_vmem(array):
    return pltpu.with_memory_space_constraint(array, pltpu.VMEM)


def gate_up(position, blocks, gate, up, loads, n, load_gate_up):
    rows, depth = blocks[0].shape
    width = gate.shape[1]
    nb, part = len(blocks), rows // n
    tile = tile_of(width, 256)
    tiles = width // tile
    kept = [gate, up] * load_gate_up + list(loads)

    def body(*refs):
        refs = list(refs)
        take = lambda count: [refs.pop(0) for _ in range(count)]
        (where,), tokens, (gate_in, up_in), load_in = take(1), take(nb), take(2), take(len(loads))
        sums, kept_out = take(n), take(len(kept))
        left, product, block_sem, tile_sem, load_sem = refs
        copies = [
            pltpu.make_async_copy(tokens[b], left.at[pl.ds(b * rows, rows)], block_sem.at[b]) for b in range(nb)
        ]
        for copy in copies:
            copy.start()
        if load_gate_up:
            weights = kept_out[:2]

            def tile_copies(t):
                columns = pl.ds(pl.multiple_of(t * tile, tile), tile)
                return [
                    pltpu.make_async_copy(source.at[:, columns], target.at[:, columns], tile_sem.at[t, k])
                    for k, (source, target) in enumerate(zip((gate_in, up_in), weights))
                ]

            def start(t, carry):
                for copy in tile_copies(t):
                    copy.start()
                return carry

            lax.fori_loop(0, tiles, start, 0)
        else:
            weights = (gate_in, up_in)
        load_copies = [
            pltpu.make_async_copy(source, target, load_sem.at[k])
            for k, (source, target) in enumerate(zip(load_in, kept_out[len(kept) - len(loads):]))
        ]
        for copy in load_copies:
            copy.start()
        for copy in copies:
            copy.wait()
        position = where[0]

        def step(t, carry):
            columns = pl.ds(pl.multiple_of(t * tile, tile), tile)
            if load_gate_up:
                for copy in tile_copies(t):
                    copy.wait()
            for k in range(2):
                product[...] = jnp.dot(left[...], weights[k][:, columns], preferred_element_type=F32)
                for j in range(n):
                    at = lax.rem(position + j, n) * part
                    parts = [
                        product[pl.ds(pl.multiple_of(b * rows + at, part), part), :] for b in range(nb)
                    ]
                    sums[j][k, :, columns] = jnp.concatenate(parts, axis=0).astype(BF16)
            return carry

        lax.fori_loop(0, tiles, step, 0)
        for copy in load_copies:
            copy.wait()

    any_spec = pl.BlockSpec(memory_space=pl.ANY)
    vmem_spec = pl.BlockSpec(memory_space=pltpu.VMEM)
    if not load_gate_up:
        gate, up = in_vmem(gate), in_vmem(up)
    moved = sum(w.size for w in kept) * 2
    outs = pl.pallas_call(
        body,
        out_shape=[jax.ShapeDtypeStruct((2, nb * part, width), BF16)] * n
        + [pltpu.VMEM(w.shape, w.dtype) for w in kept],
        in_specs=[pl.BlockSpec(memory_space=pltpu.SMEM)]
        + [any_spec] * nb
        + [any_spec if load_gate_up else vmem_spec] * 2
        + [any_spec] * len(loads),
        out_specs=[vmem_spec] * (n + len(kept)),
        scratch_shapes=[
            pltpu.VMEM((nb * rows, depth), BF16),
            pltpu.VMEM((nb * rows, tile), F32),
            pltpu.SemaphoreType.DMA((nb,)),
            pltpu.SemaphoreType.DMA((tiles, 2)),
            pltpu.SemaphoreType.DMA((max(1, len(loads)),)),
        ],
        compiler_params=pltpu.CompilerParams(vmem_limit_bytes=10 * MIB),
        cost_estimate=pl.CostEstimate(
            flops=4 * nb * rows * depth * width, bytes_accessed=moved + nb * rows * depth * 2, transcendentals=0
        ),
        name="gate_up",
    )(position, *blocks, gate, up, *loads)
    return outs[:n], outs[n:]


def down_product(position, hidden, down, nb, rows):
    n = len(hidden)
    part = rows // n
    width, depth = down.shape[1], down.shape[0]
    tile = tile_of(width, 512)

    def body(where, *refs):
        pieces, down_ref, outs = refs[:n], refs[n], refs[n + 1:n + 1 + nb]
        left, product, sem = refs[n + 1 + nb:]
        copies = [
            pltpu.make_async_copy(pieces[j], left.at[pl.ds(j * nb * part, nb * part)], sem.at[j]) for j in range(n)
        ]
        for copy in copies:
            copy.start()
        for copy in copies:
            copy.wait()
        position = where[0]

        def step(t, carry):
            columns = pl.ds(pl.multiple_of(t * tile, tile), tile)
            result = jnp.dot(left[...], down_ref[:, columns], preferred_element_type=F32)
            for j in range(n):
                at = lax.rem(position + j, n) * part
                for b in range(nb):
                    first = (j * nb + b) * part
                    product[pl.ds(pl.multiple_of(b * rows + at, part), part), :] = result[first:first + part]
            for b in range(nb):
                outs[b][:, columns] = product[b * rows:(b + 1) * rows, :].astype(BF16)
            return carry

        lax.fori_loop(0, width // tile, step, 0)

    any_spec = pl.BlockSpec(memory_space=pl.ANY)
    vmem_spec = pl.BlockSpec(memory_space=pltpu.VMEM)
    return pl.pallas_call(
        body,
        out_shape=[jax.ShapeDtypeStruct((rows, width), BF16)] * nb,
        in_specs=[pl.BlockSpec(memory_space=pltpu.SMEM)] + [any_spec] * n + [vmem_spec],
        out_specs=[vmem_spec] * nb,
        scratch_shapes=[
            pltpu.VMEM((nb * rows, depth), BF16),
            pltpu.VMEM((nb * rows, tile), F32),
            pltpu.SemaphoreType.DMA((n,)),
        ],
        compiler_params=pltpu.CompilerParams(vmem_limit_bytes=8 * MIB),
        cost_estimate=pl.CostEstimate(
            flops=2 * nb * rows * depth * width, bytes_accessed=nb * rows * width * 2, transcendentals=0
        ),
        name="down_product",
    )(position, *hidden, in_vmem(down))


def add(*terms):
    return functools.reduce(jnp.add, [t.astype(F32) for t in terms])


def shards(sizes, tokens, gate_weight, up_weight, down_weight):
    n = sizes["gz"]
    cores = 2 if sizes["gx"] % 2 == 0 else 1
    ny, nz = sizes["gx"] // cores, sizes["gy"]
    rows = tokens.shape[0]
    position = lax.axis_index("gz").astype(jnp.int32).reshape(1)

    def over_core(value):
        return lax.ppermute(value, "gx", [(i, i ^ 1) for i in range(cores * ny)])

    def over_y(value, by):
        return lax.ppermute(
            value, "gx", [(y * cores + c, (y + by) % ny * cores + c) for y in range(ny) for c in range(cores)]
        )

    def over_z(value, by):
        return lax.ppermute(value, "gy", [(z, (z + by) % nz) for z in range(nz)])

    def over_gz(value, by):
        return lax.ppermute(value, "gz", [(i, (i + by) % n) for i in range(n)])

    blocks = {}
    orders = sorted(range(nz), key=lambda z: (min(z, nz - z), z))
    for dz in orders:
        along_z = over_z(tokens, dz) if dz else tokens
        for dy in range(ny):
            one = over_y(along_z, dy) if dy else along_z
            blocks[dy, dz] = [one] + ([over_core(one)] if cores == 2 else [])

    pieces = [[(dy, 0)] for dy in range(ny)]
    pieces = pieces[:1] + [[(dy, dz) for dy in range(ny)] for dz in orders[1:]] + pieces[1:]

    weights = [gate_weight, up_weight, down_weight]
    hiddens = []
    for index, piece in enumerate(pieces):
        arrays = [block for where in piece for block in blocks[where]]
        sums, kept = gate_up(
            position, arrays, weights[0], weights[1], [down_weight] * (index == 1), n, index == 0
        )
        if index == 0:
            weights[:2] = kept
        if index == 1:
            weights[2:] = kept
        arrived = [over_gz(sums[j], j) for j in range(1, n)]
        both = add(sums[0], *arrived)
        own = (jax.nn.silu(both[0]) * both[1]).astype(BF16)
        hiddens.append([own] + [over_gz(own, -j) for j in range(1, n)])

    totals = {}
    for piece, hidden in zip(pieces, hiddens):
        partial = down_product(position, hidden, weights[2], len(piece) * cores, rows)
        for index, where in enumerate(piece):
            mine = partial[index * cores]
            totals[where] = [mine] + ([over_core(partial[index * cores + 1])] if cores == 2 else [])

    finals = []
    for dz in orders:
        terms = list(totals[0, dz])
        for dy in range(1, ny):
            terms.append(over_y(add(*totals[dy, dz]).astype(BF16), -dy))
        if dz:
            finals.append(over_z(add(*terms).astype(BF16), -dz))
        else:
            finals.extend(terms)
    return add(*finals).astype(BF16)


def solution(mesh):
    sizes = dict(mesh.shape)
    return jax.shard_map(
        functools.partial(shards, sizes),
        mesh=mesh,
        in_specs=(
            P(("gx", "gy"), "gz"),
            P("gz", ("gx", "gy")),
            P("gz", ("gx", "gy")),
            P(("gx", "gy"), "gz"),
        ),
        out_specs=P(("gx", "gy"), "gz"),
        check_vma=False,
    )
```

```python
import functools

import jax
import jax.numpy as jnp
from jax import lax
from jax.experimental import pallas as pl
from jax.experimental.pallas import tpu as pltpu
from jax.sharding import PartitionSpec as P

BF16 = jnp.bfloat16
F32 = jnp.float32
MIB = 1 << 20
FLOPS = [1, 1, 1]


def cost(kind):
    return pl.CostEstimate(flops=FLOPS[kind], bytes_accessed=1, transcendentals=0)


def tile_of(width, most):
    return max(t for t in range(128, most + 1, 128) if width % t == 0)


def in_vmem(array):
    return pltpu.with_memory_space_constraint(array, pltpu.VMEM)


def in_hbm(array):
    return pltpu.with_memory_space_constraint(array, pltpu.HBM)


SLAB = 512
SLOTS = 3
LIMIT = 12 * MIB


def first_gate_up(position, pieces, rows, gate, up, n):
    depth, width = gate.shape
    starts = [0]
    for piece in pieces:
        starts.append(starts[-1] + piece.shape[0])
    count = len(pieces)
    nb, part = starts[-1] // rows, rows // n
    tile = tile_of(width, 256)
    slab = tile_of(depth, SLAB)
    slabs = depth // slab
    slots = min(slabs, SLOTS)

    def body(where, *refs):
        tokens, gate_in, up_in, sums, gate_out = refs[:count], refs[count], refs[count + 1], refs[count + 2:count + 2 + n], refs[count + 2 + n]
        left, totals, up_slots, block_sem, gate_sem, up_sem = refs[count + 3 + n:]

        def slab_copy(k, s):
            at = pl.ds(s * slab, slab)
            if k:
                return pltpu.make_async_copy(up_in.at[at], up_slots.at[s % slots], up_sem.at[s % slots])
            return pltpu.make_async_copy(gate_in.at[at], gate_out.at[at], gate_sem.at[s])

        copies = [
            pltpu.make_async_copy(tokens[b], left.at[starts[b]:starts[b + 1]], block_sem.at[b]) for b in range(count)
        ]
        for copy in copies:
            copy.start()
        for s in range(slots):
            for k in range(2):
                slab_copy(k, s).start()
        for copy in copies:
            copy.wait()
        position = where[0]
        for s in range(slabs):
            for k in range(2):
                slab_copy(k, s).wait()
                right = up_slots.at[s % slots] if k else gate_out.at[pl.ds(s * slab, slab)]
                for t in range(width // tile):
                    columns = pl.ds(t * tile, tile)
                    term = jnp.dot(left[:, pl.ds(s * slab, slab)], right[:, columns], preferred_element_type=F32)
                    totals[k, :, columns] = term + totals[k, :, columns] if s else term
                if s + slots < slabs:
                    slab_copy(k, s + slots).start()
        for k in range(2):
            for j in range(n):
                at = lax.rem(position + j, n) * part
                parts = [totals[k, pl.ds(pl.multiple_of(b * rows + at, part), part), :] for b in range(nb)]
                sums[j][k] = jnp.concatenate(parts, axis=0).astype(BF16)

    any_spec = pl.BlockSpec(memory_space=pl.ANY)
    vmem_spec = pl.BlockSpec(memory_space=pltpu.VMEM)
    outs = pl.pallas_call(
        body,
        out_shape=[jax.ShapeDtypeStruct((2, nb * part, width), BF16)] * n + [pltpu.VMEM(gate.shape, BF16)],
        in_specs=[pl.BlockSpec(memory_space=pltpu.SMEM)] + [any_spec] * (count + 2),
        out_specs=[vmem_spec] * (n + 1),
        scratch_shapes=[
            pltpu.VMEM((nb * rows, depth), BF16),
            pltpu.VMEM((2, nb * rows, width), F32),
            pltpu.VMEM((slots, slab, width), BF16),
            pltpu.SemaphoreType.DMA((count,)),
            pltpu.SemaphoreType.DMA((slabs,)),
            pltpu.SemaphoreType.DMA((slots,)),
        ],
        compiler_params=pltpu.CompilerParams(vmem_limit_bytes=LIMIT),
        cost_estimate=cost(0),
        name="first_gate_up",
    )(position, *pieces, in_hbm(gate), in_hbm(up))
    return outs[:n], outs[n]


def load(array):
    def body(source, target, sem):
        copy = pltpu.make_async_copy(source, target, sem.at[0])
        copy.start()
        copy.wait()

    return pl.pallas_call(
        body,
        out_shape=pltpu.VMEM(array.shape, array.dtype),
        in_specs=[pl.BlockSpec(memory_space=pl.ANY)],
        out_specs=pl.BlockSpec(memory_space=pltpu.VMEM),
        scratch_shapes=[pltpu.SemaphoreType.DMA((1,))],
        compiler_params=pltpu.CompilerParams(vmem_limit_bytes=LIMIT),
        cost_estimate=cost(2),
        name="load",
    )(in_hbm(array))


def gate_up(position, pieces, rows, gate, up, n, apart):
    depth, width = gate.shape
    starts = [0]
    for piece in pieces:
        starts.append(starts[-1] + piece.shape[0])
    count = len(pieces)
    nb, part = starts[-1] // rows, rows // n
    tile = tile_of(width, 256)
    tiles = width // tile
    slots = min(tiles, 2)

    whole = jax.ShapeDtypeStruct((2, nb * part, width), BF16)
    half = jax.ShapeDtypeStruct((1, nb * part, width), BF16)
    outs = [whole] + ([half] * 2 if apart else [whole]) * (n - 1)

    def body(where, *refs):
        tokens, gate_ref, up_in = refs[:count], refs[count], refs[count + 1]
        results = refs[count + 2:count + 2 + len(outs)]
        left, product, up_slots, block_sem, up_sem = refs[count + 2 + len(outs):]
        copies = [
            pltpu.make_async_copy(tokens[b], left.at[starts[b]:starts[b + 1]], block_sem.at[b]) for b in range(count)
        ]
        for copy in copies:
            copy.start()

        def up_copy(t):
            return pltpu.make_async_copy(
                up_in.at[:, pl.ds(t * tile, tile)], up_slots.at[t % slots], up_sem.at[t % slots]
            )

        for t in range(slots):
            up_copy(t).start()
        for copy in copies:
            copy.wait()
        position = where[0]

        def put(k, columns, right):
            product[...] = jnp.dot(left[...], right, preferred_element_type=F32)
            for j in range(n):
                at = lax.rem(position + j, n) * part
                parts = [product[pl.ds(pl.multiple_of(b * rows + at, part), part), :] for b in range(nb)]
                value = jnp.concatenate(parts, axis=0).astype(BF16)
                if j and apart:
                    results[2 * j - 1 + k][0, :, columns] = value
                else:
                    results[j][k, :, columns] = value

        for t in range(tiles):
            columns = pl.ds(t * tile, tile)
            put(0, columns, gate_ref[:, columns])
            up_copy(t).wait()
            put(1, columns, up_slots[t % slots])
            if t + slots < tiles:
                up_copy(t + slots).start()

    any_spec = pl.BlockSpec(memory_space=pl.ANY)
    vmem_spec = pl.BlockSpec(memory_space=pltpu.VMEM)
    return pl.pallas_call(
        body,
        out_shape=outs,
        in_specs=[pl.BlockSpec(memory_space=pltpu.SMEM)] + [any_spec] * count + [vmem_spec, any_spec],
        out_specs=[vmem_spec] * len(outs),
        scratch_shapes=[
            pltpu.VMEM((nb * rows, depth), BF16),
            pltpu.VMEM((nb * rows, tile), F32),
            pltpu.VMEM((slots, depth, tile), BF16),
            pltpu.SemaphoreType.DMA((count,)),
            pltpu.SemaphoreType.DMA((slots,)),
        ],
        compiler_params=pltpu.CompilerParams(vmem_limit_bytes=LIMIT),
        cost_estimate=cost(0),
        name="gate_up",
    )(position, *pieces, in_vmem(gate), in_hbm(up))


def down_product(position, hidden, down, chips, cores, rows, span):
    n = len(hidden)
    part = rows // n
    nb = chips * cores
    depth, width = down.shape
    tile = tile_of(width, 512)
    tiles = width // tile
    span = span if tiles % span == 0 else 1
    tiles_each = tiles // span
    others = (cores - 1) * span

    def body(where, *refs):
        pieces, right, outs = refs[:n], refs[n], refs[n + 1:n + 2 + others]
        left, product, sem = refs[n + 2 + others:]
        copies = [
            pltpu.make_async_copy(pieces[j], left.at[pl.ds(j * nb * part, nb * part)], sem.at[j]) for j in range(n)
        ]
        for copy in copies:
            copy.start()
        for copy in copies:
            copy.wait()
        position = where[0]

        def step(group, t):
            columns = pl.ds(pl.multiple_of((group * tiles_each + t) * tile, tile), tile)
            here = pl.ds(pl.multiple_of(t * tile, tile), tile)
            result = jnp.dot(left[...], right[:, columns], preferred_element_type=F32)
            for j in range(n):
                at = lax.rem(position + j, n) * part
                for b in range(nb):
                    first = (j * nb + b) * part
                    product[pl.ds(pl.multiple_of(b * rows + at, part), part), :] = result[first:first + part]
            for b in range(nb):
                at = b // cores * rows
                value = product[b * rows:(b + 1) * rows, :].astype(BF16)
                if b % cores:
                    outs[1 + group][at:at + rows, here] = value
                else:
                    outs[0][at:at + rows, columns] = value

        for group in range(span):
            lax.fori_loop(0, tiles_each, lambda t, carry: step(group, t), None)

    any_spec = pl.BlockSpec(memory_space=pl.ANY)
    vmem_spec = pl.BlockSpec(memory_space=pltpu.VMEM)
    outs = pl.pallas_call(
        body,
        out_shape=[jax.ShapeDtypeStruct((chips * rows, width), BF16)]
        + [jax.ShapeDtypeStruct((chips * rows, width // span), BF16)] * others,
        in_specs=[pl.BlockSpec(memory_space=pltpu.SMEM)] + [any_spec] * n + [vmem_spec],
        out_specs=[vmem_spec] * (1 + others),
        scratch_shapes=[
            pltpu.VMEM((nb * rows, depth), BF16),
            pltpu.VMEM((nb * rows, tile), F32),
            pltpu.SemaphoreType.DMA((n,)),
        ],
        compiler_params=pltpu.CompilerParams(vmem_limit_bytes=LIMIT),
        cost_estimate=cost(1),
        name="down_product",
    )(position, *hidden, in_vmem(down))
    return outs[0], outs[1:]


def elementwise(name, function, outs, *terms):
    count = len(terms)

    def body(*refs):
        results = function(*[ref[...].astype(F32) for ref in refs[:count]])
        for ref, result in zip(refs[count:], results):
            ref[...] = result.astype(ref.dtype)

    spec = pl.BlockSpec(memory_space=pltpu.VMEM)
    return pl.pallas_call(
        body,
        out_shape=outs,
        in_specs=[spec] * count,
        out_specs=[spec] * len(outs),
        compiler_params=pltpu.CompilerParams(vmem_limit_bytes=LIMIT),
        cost_estimate=cost(2),
        name=name,
    )(*terms)


def add(*terms):
    return elementwise(
        "add", lambda *t: [functools.reduce(jnp.add, t)], [jax.ShapeDtypeStruct(terms[0].shape, BF16)], *terms
    )[0]


def split(array, count):
    rows = array.shape[0] // count
    outs = [jax.ShapeDtypeStruct((rows,) + array.shape[1:], BF16)] * count
    return elementwise("split", lambda value: [value[k * rows:(k + 1) * rows] for k in range(count)], outs, array)


def add_blocks(count, mine, *theirs):
    rows, width = mine.shape[0] // count, mine.shape[1]

    def function(total, *parts):
        if parts:
            total = total + jnp.concatenate(parts, axis=1)
        return [total[k * rows:(k + 1) * rows] for k in range(count)]

    return elementwise("add_blocks", function, [jax.ShapeDtypeStruct((rows, width), BF16)] * count, mine, *theirs)


def hidden_of(mine, *theirs):
    def function(both, *terms):
        terms = list(terms)
        while terms:
            term = terms.pop(0)
            both = both + (term if term.shape[0] == 2 else jnp.concatenate([term, terms.pop(0)], axis=0))
        return [jax.nn.silu(both[0]) * both[1]]

    return elementwise("hidden", function, [jax.ShapeDtypeStruct(mine.shape[1:], BF16)], mine, *theirs)[0]


def shards(sizes, tokens, gate_weight, up_weight, down_weight):
    n = sizes["gz"]
    cores = 2 if sizes["gx"] % 2 == 0 else 1
    ny, nz = sizes["gx"] // cores, sizes["gy"]
    rows = tokens.shape[0]
    position = lax.axis_index("gz").astype(jnp.int32).reshape(1)

    def over_core(value):
        return lax.ppermute(value, "gx", [(i, i ^ 1) for i in range(cores * ny)])

    def over_y(value, by):
        return lax.ppermute(
            value, "gx", [(y * cores + c, (y + by) % ny * cores + c) for y in range(ny) for c in range(cores)]
        )

    def over_z(value, by):
        return lax.ppermute(value, "gy", [(z, (z + by) % nz) for z in range(nz)])

    def over_gz(value, by):
        return lax.ppermute(value, "gz", [(i, (i + by) % n) for i in range(n)])

    def home(value, dy, dz):
        pairs = []
        for y in range(ny):
            for c in range(cores):
                for z in range(nz):
                    source = (y * cores + c) * nz + z
                    pairs.append((source, ((y - dy) % ny * cores + c) * nz + (z - dz) % nz))
        return lax.ppermute(value, ("gx", "gy"), pairs)

    last, settled = [], []

    def ordered(call, *arrays):
        extra = [blocks_of[key] for key in settled]
        if last or extra:
            arrays, values, _ = lax.optimization_barrier((arrays, extra, list(last)))
            blocks_of.update(zip(settled, values))
        settled.clear()
        result = call(*arrays)
        last[:] = [jax.tree.leaves(result)[0]]
        return result

    def settle(key):
        blocks_of[key] = lax.optimization_barrier((blocks_of[key], list(last)))[0]
        settled.append(key)

    others = sorted(range(1, nz), key=lambda z: (min(z, nz - z), z))
    blocks_of = {}
    gate, up, down = gate_weight, up_weight, None
    sums, hiddens, partials, totals, arriving = {}, {}, {}, {}, {}

    def fetch_core(dy, dz):
        if cores == 2:
            (block,) = blocks_of[dy, dz]
            halves = split(block, 2) if (dy, dz) in cut and rows % 32 == 0 else [block]
            blocks_of["core", dy, dz] = [over_core(half) for half in halves]

    def fetch_y(dy, dz):
        blocks_of[dy, dz] = [over_y(half, dy) for half in blocks_of[0, dz]]

    def fetch_z(dz, via=0):
        blocks_of[0, dz] = [over_z(half, dz - via) for half in blocks_of[0, via]]

    def step_gate_up(p):
        nonlocal gate
        arrays = []
        for where in pieces[p]:
            arrays += blocks_of[where] + (blocks_of["core", *where] if cores == 2 else [])
        if p == 0:
            results, gate = ordered(lambda *a: first_gate_up(position, list(a), rows, gate, up, n), *arrays)
        else:
            results = ordered(lambda *a: gate_up(position, list(a), rows, gate, up, n, p in apart), *arrays)
        sums[p] = results
        if p not in held:
            step_send(p)

    def step_send(p):
        mine, *theirs = sums[p]
        if p in held:
            theirs, _ = lax.optimization_barrier((theirs, list(last)))
        each = len(theirs) // (n - 1)
        sums[p] = [mine] + [over_gz(value, 1 + k // each) for k, value in enumerate(theirs)]

    def step_load():
        nonlocal down
        down = ordered(load, down_weight)

    def step_hidden(p):
        own = ordered(hidden_of, *sums[p])
        hiddens[p] = own
        blocks_of["hidden", p] = [over_gz(own, -j) for j in range(1, n)]

    def step_down(p):
        mine, theirs = ordered(
            lambda *a: down_product(position, list(a), down, len(pieces[p]), cores, rows, spans[p]),
            hiddens[p],
            *blocks_of["hidden", p],
        )
        partials[p] = [mine] + [over_core(t) for t in theirs]

    def step_total(p):
        results = ordered(lambda *a: add_blocks(len(pieces[p]), *a), *partials[p])
        for (dy, dz), result in zip(pieces[p], results):
            if (dy, dz) in straight and (dy or dz):
                blocks_of["home", dy, dz] = home(result, dy, dz)
            elif dy:
                blocks_of["sum", dy, dz] = over_y(result, -dy)
            else:
                blocks_of["sum", dy, dz] = result

    def step_y(dz):
        total = ordered(add, *[blocks_of["sum", dy, dz] for dy in range(ny) if (dy, dz) not in straight])
        blocks_of["home", 0, dz] = over_z(total, -dz)

    F, Z, C, S = fetch_y, fetch_z, fetch_core, settle
    G, R, H, D, T, Y, L = step_gate_up, step_send, step_hidden, step_down, step_total, step_y, step_load
    blocks_of[0, 0] = [tokens]
    if ny == 2 and nz == 4 and cores == 2:
        pieces = [[(0, 0)], [(1, 0), (0, 1)], [(1, 1), (0, 3)], [(0, 2), (1, 2)], [(1, 3)]]
        straight = [(0, 1), (1, 1), (0, 3), (1, 3)]
        held, apart, spans = [], [4], [2, 2, 4, 2, 2]
        cut = []
        plan = [
            (C, 0, 0), (Z, 1), (F, 1, 0), (Z, 3), (G, 0), (F, 1, 3), (S, (1, 0)), (C, 0, 1), (C, 1, 0), (F, 1, 1),
            (G, 1), (H, 0), (S, (0, 3)), (S, (1, 1)), (Z, 2, 1), (C, 0, 3), (C, 1, 1), (F, 1, 2), (G, 2), (C, 0, 2),
            (H, 1), (L,), (S, (1, 2)), (C, 1, 2), (D, 0), (T, 0), (S, (0, 2)), (G, 3), (S, (1, 3)), (H, 2),
            (C, 1, 3), (D, 1), (T, 1), (G, 4), (H, 3), (S, ("sum", 1, 0)), (S, (0, 3)), (D, 2), (S, ("home", 0, 1)),
            (S, ("core", 0, 2)), (D, 3), (T, 2), (T, 3), (H, 4), (S, ("home", 1, 1)), (D, 4), (S, (1, 0)),
            (S, ("home", 0, 3)), (S, ("sum", 1, 2)), (Y, 2), (S, ("core", 1, 1)), (T, 4),
        ]
    else:
        pieces = [[(dy, dz)] for dz in [0] + others for dy in range(ny)]
        straight = []
        held, apart, cut, spans = [], [], [], [1] * len(pieces)
        count = len(pieces)
        plan = [(F, dy, 0) for dy in range(1, ny)]
        for dz in others:
            plan += [(Z, dz)] + [(F, dy, dz) for dy in range(1, ny)]
        plan += [(C, *where) for piece in pieces for where in piece] + [(G, 0), (L,)]
        for p in range(count):
            plan += [(G, p + 1)] * (p + 1 < count) + [(H, p)] + [(D, p - 1), (T, p - 1)] * (p > 0)
        plan += [(D, count - 1), (T, count - 1)] + [(Y, dz) for dz in others]
    for step, *arguments in plan:
        step(*arguments)
    finals = [blocks_of["sum", dy, 0] for dy in range(ny)]
    finals += [value for key, value in blocks_of.items() if key[0] == "home"]
    return ordered(add, *finals)


def solution(mesh):
    sizes = dict(mesh.shape)
    return jax.shard_map(
        functools.partial(shards, sizes),
        mesh=mesh,
        in_specs=(
            P(("gx", "gy"), "gz"),
            P("gz", ("gx", "gy")),
            P("gz", ("gx", "gy")),
            P(("gx", "gy"), "gz"),
        ),
        out_specs=P(("gx", "gy"), "gz"),
        check_vma=False,
    )
```

```python
import functools

import jax
import jax.numpy as jnp
from jax import lax
from jax.experimental import pallas as pl
from jax.experimental.pallas import tpu as pltpu
from jax.sharding import PartitionSpec as P

BF16 = jnp.bfloat16
F32 = jnp.float32
MIB = 1 << 20
FLOPS = [1, 1, 2000000000]


def cost(kind):
    return pl.CostEstimate(flops=FLOPS[kind], bytes_accessed=1, transcendentals=0)


def tile_of(width, most):
    return max(t for t in range(128, most + 1, 128) if width % t == 0)


def in_vmem(array):
    return pltpu.with_memory_space_constraint(array, pltpu.VMEM)


def in_hbm(array):
    return pltpu.with_memory_space_constraint(array, pltpu.HBM)


SLAB = 512
SLOTS = 3
LIMIT = 15 * MIB


def first_gate_up(position, pieces, rows, gate, up, n):
    depth, width = gate.shape
    starts = [0]
    for piece in pieces:
        starts.append(starts[-1] + piece.shape[0])
    count = len(pieces)
    nb, part = starts[-1] // rows, rows // n
    tile = tile_of(width, 256)
    slab = tile_of(depth, SLAB)
    slabs = depth // slab
    slots = min(slabs, SLOTS)

    def body(where, *refs):
        tokens, gate_in, up_in, sums, gate_out = refs[:count], refs[count], refs[count + 1], refs[count + 2:count + 2 + n], refs[count + 2 + n]
        left, totals, up_slots, block_sem, gate_sem, up_sem = refs[count + 3 + n:]

        def slab_copy(k, s):
            at = pl.ds(s * slab, slab)
            if k:
                return pltpu.make_async_copy(up_in.at[at], up_slots.at[s % slots], up_sem.at[s % slots])
            return pltpu.make_async_copy(gate_in.at[at], gate_out.at[at], gate_sem.at[s])

        copies = [
            pltpu.make_async_copy(tokens[b], left.at[starts[b]:starts[b + 1]], block_sem.at[b]) for b in range(count)
        ]
        for copy in copies:
            copy.start()
        for s in range(slots):
            for k in range(2):
                slab_copy(k, s).start()
        for copy in copies:
            copy.wait()
        position = where[0]
        for s in range(slabs):
            for k in range(2):
                slab_copy(k, s).wait()
                right = up_slots.at[s % slots] if k else gate_out.at[pl.ds(s * slab, slab)]
                for t in range(width // tile):
                    columns = pl.ds(t * tile, tile)
                    term = jnp.dot(left[:, pl.ds(s * slab, slab)], right[:, columns], preferred_element_type=F32)
                    totals[k, :, columns] = term + totals[k, :, columns] if s else term
                if s + slots < slabs:
                    slab_copy(k, s + slots).start()
        for k in range(2):
            for j in range(n):
                at = lax.rem(position + j, n) * part
                parts = [totals[k, pl.ds(pl.multiple_of(b * rows + at, part), part), :] for b in range(nb)]
                sums[j][k] = jnp.concatenate(parts, axis=0).astype(BF16)

    any_spec = pl.BlockSpec(memory_space=pl.ANY)
    vmem_spec = pl.BlockSpec(memory_space=pltpu.VMEM)
    outs = pl.pallas_call(
        body,
        out_shape=[jax.ShapeDtypeStruct((2, nb * part, width), BF16)] * n + [pltpu.VMEM(gate.shape, BF16)],
        in_specs=[pl.BlockSpec(memory_space=pltpu.SMEM)] + [any_spec] * (count + 2),
        out_specs=[vmem_spec] * (n + 1),
        scratch_shapes=[
            pltpu.VMEM((nb * rows, depth), BF16),
            pltpu.VMEM((2, nb * rows, width), F32),
            pltpu.VMEM((slots, slab, width), BF16),
            pltpu.SemaphoreType.DMA((count,)),
            pltpu.SemaphoreType.DMA((slabs,)),
            pltpu.SemaphoreType.DMA((slots,)),
        ],
        compiler_params=pltpu.CompilerParams(vmem_limit_bytes=LIMIT),
        cost_estimate=cost(0),
        name="first_gate_up",
    )(position, *pieces, in_hbm(gate), in_hbm(up))
    return outs[:n], outs[n]


def load(array):
    def body(source, target, sem):
        copy = pltpu.make_async_copy(source, target, sem.at[0])
        copy.start()
        copy.wait()

    return pl.pallas_call(
        body,
        out_shape=pltpu.VMEM(array.shape, array.dtype),
        in_specs=[pl.BlockSpec(memory_space=pl.ANY)],
        out_specs=pl.BlockSpec(memory_space=pltpu.VMEM),
        scratch_shapes=[pltpu.SemaphoreType.DMA((1,))],
        compiler_params=pltpu.CompilerParams(vmem_limit_bytes=LIMIT),
        cost_estimate=cost(2),
        name="load",
    )(in_hbm(array))


def gate_up(position, pieces, rows, gate, up, n, apart):
    depth, width = gate.shape
    starts = [0]
    for piece in pieces:
        starts.append(starts[-1] + piece.shape[0])
    count = len(pieces)
    nb, part = starts[-1] // rows, rows // n
    tile = tile_of(width, 256)
    tiles = width // tile
    slots = min(tiles, 3)

    whole = jax.ShapeDtypeStruct((2, nb * part, width), BF16)
    half = jax.ShapeDtypeStruct((1, nb * part, width), BF16)
    outs = [whole] + ([half] * 2 if apart else [whole]) * (n - 1)

    def body(where, *refs):
        tokens, gate_ref, up_in = refs[:count], refs[count], refs[count + 1]
        results = refs[count + 2:count + 2 + len(outs)]
        left, product, up_slots, block_sem, up_sem = refs[count + 2 + len(outs):]
        copies = [
            pltpu.make_async_copy(tokens[b], left.at[starts[b]:starts[b + 1]], block_sem.at[b]) for b in range(count)
        ]
        for copy in copies:
            copy.start()

        def up_copy(t):
            return pltpu.make_async_copy(
                up_in.at[:, pl.ds(t * tile, tile)], up_slots.at[t % slots], up_sem.at[t % slots]
            )

        for t in range(slots):
            up_copy(t).start()
        for copy in copies:
            copy.wait()
        position = where[0]

        def put(k, columns, right):
            product[...] = jnp.dot(left[...], right, preferred_element_type=F32)
            for j in range(n):
                at = lax.rem(position + j, n) * part
                parts = [product[pl.ds(pl.multiple_of(b * rows + at, part), part), :] for b in range(nb)]
                value = jnp.concatenate(parts, axis=0).astype(BF16)
                if j and apart:
                    results[2 * j - 1 + k][0, :, columns] = value
                else:
                    results[j][k, :, columns] = value

        for t in range(tiles):
            columns = pl.ds(t * tile, tile)
            put(0, columns, gate_ref[:, columns])
            up_copy(t).wait()
            put(1, columns, up_slots[t % slots])
            if t + slots < tiles:
                up_copy(t + slots).start()

    any_spec = pl.BlockSpec(memory_space=pl.ANY)
    vmem_spec = pl.BlockSpec(memory_space=pltpu.VMEM)
    return pl.pallas_call(
        body,
        out_shape=outs,
        in_specs=[pl.BlockSpec(memory_space=pltpu.SMEM)] + [any_spec] * count + [vmem_spec, any_spec],
        out_specs=[vmem_spec] * len(outs),
        scratch_shapes=[
            pltpu.VMEM((nb * rows, depth), BF16),
            pltpu.VMEM((nb * rows, tile), F32),
            pltpu.VMEM((slots, depth, tile), BF16),
            pltpu.SemaphoreType.DMA((count,)),
            pltpu.SemaphoreType.DMA((slots,)),
        ],
        compiler_params=pltpu.CompilerParams(vmem_limit_bytes=LIMIT),
        cost_estimate=cost(0),
        name="gate_up",
    )(position, *pieces, in_vmem(gate), in_hbm(up))


def down_product(position, hidden, down, chips, cores, rows, span):
    n = len(hidden)
    part = rows // n
    nb = chips * cores
    depth, width = down.shape
    tile = tile_of(width, 512)
    tiles = width // tile
    span = span if tiles % span == 0 else 1
    tiles_each = tiles // span
    others = (cores - 1) * span

    def body(where, *refs):
        pieces, right, outs = refs[:n], refs[n], refs[n + 1:n + 2 + others]
        left, product, sem = refs[n + 2 + others:]
        copies = [
            pltpu.make_async_copy(pieces[j], left.at[pl.ds(j * nb * part, nb * part)], sem.at[j]) for j in range(n)
        ]
        for copy in copies:
            copy.start()
        for copy in copies:
            copy.wait()
        position = where[0]

        def step(group, t):
            columns = pl.ds(pl.multiple_of((group * tiles_each + t) * tile, tile), tile)
            here = pl.ds(pl.multiple_of(t * tile, tile), tile)
            result = jnp.dot(left[...], right[:, columns], preferred_element_type=F32)
            for j in range(n):
                at = lax.rem(position + j, n) * part
                for b in range(nb):
                    first = (j * nb + b) * part
                    product[pl.ds(pl.multiple_of(b * rows + at, part), part), :] = result[first:first + part]
            for b in range(nb):
                at = b // cores * rows
                value = product[b * rows:(b + 1) * rows, :].astype(BF16)
                if b % cores:
                    outs[1 + group][at:at + rows, here] = value
                else:
                    outs[0][at:at + rows, columns] = value

        for group in range(span):
            lax.fori_loop(0, tiles_each, lambda t, carry: step(group, t), None)

    any_spec = pl.BlockSpec(memory_space=pl.ANY)
    vmem_spec = pl.BlockSpec(memory_space=pltpu.VMEM)
    outs = pl.pallas_call(
        body,
        out_shape=[jax.ShapeDtypeStruct((chips * rows, width), BF16)]
        + [jax.ShapeDtypeStruct((chips * rows, width // span), BF16)] * others,
        in_specs=[pl.BlockSpec(memory_space=pltpu.SMEM)] + [any_spec] * n + [vmem_spec],
        out_specs=[vmem_spec] * (1 + others),
        scratch_shapes=[
            pltpu.VMEM((nb * rows, depth), BF16),
            pltpu.VMEM((nb * rows, tile), F32),
            pltpu.SemaphoreType.DMA((n,)),
        ],
        compiler_params=pltpu.CompilerParams(vmem_limit_bytes=LIMIT),
        cost_estimate=cost(1),
        name="down_product",
    )(position, *hidden, in_vmem(down))
    return outs[0], outs[1:]


def elementwise(name, function, outs, *terms):
    count = len(terms)

    def body(*refs):
        results = function(*[ref[...].astype(F32) for ref in refs[:count]])
        for ref, result in zip(refs[count:], results):
            ref[...] = result.astype(ref.dtype)

    spec = pl.BlockSpec(memory_space=pltpu.VMEM)
    return pl.pallas_call(
        body,
        out_shape=outs,
        in_specs=[spec] * count,
        out_specs=[spec] * len(outs),
        compiler_params=pltpu.CompilerParams(vmem_limit_bytes=LIMIT),
        cost_estimate=cost(2),
        name=name,
    )(*terms)


def add(*terms):
    counts = [len(term) for term in terms]

    def function(*parts):
        parts = list(parts)
        wholes = [[parts.pop(0) for _ in range(count)] for count in counts]
        return [functools.reduce(jnp.add, [jnp.concatenate(w, axis=0) if len(w) > 1 else w[0] for w in wholes])]

    rows = sum(part.shape[0] for part in terms[0])
    out = jax.ShapeDtypeStruct((rows,) + terms[0][0].shape[1:], BF16)
    return elementwise("add", function, [out], *[part for term in terms for part in term])[0]


def split(array, count):
    rows = array.shape[0] // count
    outs = [jax.ShapeDtypeStruct((rows,) + array.shape[1:], BF16)] * count
    return elementwise("split", lambda value: [value[k * rows:(k + 1) * rows] for k in range(count)], outs, array)


def add_blocks(cuts, mine, *theirs):
    rows, width = mine.shape[0] // len(cuts), mine.shape[1]
    bounds = [
        (k * rows + j * rows // cut, k * rows + (j + 1) * rows // cut) for k, cut in enumerate(cuts) for j in range(cut)
    ]

    def function(total, *parts):
        if parts:
            total = total + jnp.concatenate(parts, axis=1)
        return [total[first:end] for first, end in bounds]

    outs = [jax.ShapeDtypeStruct((end - first, width), BF16) for first, end in bounds]
    results = list(elementwise("add_blocks", function, outs, mine, *theirs))
    return [[results.pop(0) for _ in range(cut)] for cut in cuts]


def hidden_of(mine, *theirs):
    def function(both, *terms):
        terms = list(terms)
        while terms:
            term = terms.pop(0)
            both = both + (term if term.shape[0] == 2 else jnp.concatenate([term, terms.pop(0)], axis=0))
        return [jax.nn.silu(both[0]) * both[1]]

    return elementwise("hidden", function, [jax.ShapeDtypeStruct(mine.shape[1:], BF16)], mine, *theirs)[0]


def shards(sizes, tokens, gate_weight, up_weight, down_weight):
    n = sizes["gz"]
    cores = 2 if sizes["gx"] % 2 == 0 else 1
    ny, nz = sizes["gx"] // cores, sizes["gy"]
    rows = tokens.shape[0]
    position = lax.axis_index("gz").astype(jnp.int32).reshape(1)

    def over_core(value):
        return lax.ppermute(value, "gx", [(i, i ^ 1) for i in range(cores * ny)])

    def over_y(value, by):
        return lax.ppermute(
            value, "gx", [(y * cores + c, (y + by) % ny * cores + c) for y in range(ny) for c in range(cores)]
        )

    def over_z(value, by):
        return lax.ppermute(value, "gy", [(z, (z + by) % nz) for z in range(nz)])

    def over_gz(value, by):
        return lax.ppermute(value, "gz", [(i, (i + by) % n) for i in range(n)])

    def home(value, dy, dz):
        pairs = []
        for y in range(ny):
            for c in range(cores):
                for z in range(nz):
                    source = (y * cores + c) * nz + z
                    pairs.append((source, ((y - dy) % ny * cores + c) * nz + (z - dz) % nz))
        return lax.ppermute(value, ("gx", "gy"), pairs)

    last, settled, early = [], [], []

    def ordered(call, *arrays):
        extra = [blocks_of[key] for key in settled]
        if last or extra:
            arrays, values, _ = lax.optimization_barrier((arrays, extra, list(last)))
            blocks_of.update(zip(settled, values))
        settled.clear()
        result = call(*arrays)
        last[:] = [jax.tree.leaves(result)[0]]
        return result

    def settle(key):
        blocks_of[key] = lax.optimization_barrier((blocks_of[key], list(last)))[0]
        settled.append(key)

    others = sorted(range(1, nz), key=lambda z: (min(z, nz - z), z))
    blocks_of = {}
    gate, up, down = gate_weight, up_weight, None
    sums, hiddens, partials, totals, arriving = {}, {}, {}, {}, {}

    def fetch_core(dy, dz):
        if cores == 2:
            (block,) = blocks_of[dy, dz]
            halves = split(block, 2) if (dy, dz) in cut and rows % 32 == 0 else [block]
            blocks_of["core", dy, dz] = [over_core(half) for half in halves]

    def fetch_y(dy, dz):
        blocks_of[dy, dz] = [over_y(half, dy) for half in blocks_of[0, dz]]

    def fetch_z(dz, via=0):
        blocks_of[0, dz] = [over_z(half, dz - via) for half in blocks_of[0, via]]

    def step_gate_up(p):
        nonlocal gate
        arrays = []
        for where in pieces[p]:
            arrays += blocks_of[where] + (blocks_of["core", *where] if cores == 2 else [])
        if p == 0 and not early:
            results, gate = ordered(lambda *a: first_gate_up(position, list(a), rows, gate, up, n), *arrays)
        else:
            results = ordered(lambda *a: gate_up(position, list(a), rows, gate, up, n, p in apart), *arrays)
        sums[p] = results
        if p not in held:
            step_send(p)

    def step_send(p):
        mine, *theirs = sums[p]
        if p in held:
            theirs, _ = lax.optimization_barrier((theirs, list(last)))
        each = len(theirs) // (n - 1)
        sums[p] = [mine] + [over_gz(value, 1 + k // each) for k, value in enumerate(theirs)]

    def step_load():
        nonlocal down
        down = ordered(load, down_weight)

    def step_early():
        nonlocal gate
        gate = ordered(load, gate_weight)
        early.append(True)

    def step_hidden(p):
        own = ordered(hidden_of, *sums[p])
        hiddens[p] = own
        blocks_of["hidden", p] = [over_gz(own, -j) for j in range(1, n)]

    def step_down(p):
        mine, theirs = ordered(
            lambda *a: down_product(position, list(a), down, len(pieces[p]), cores, rows, spans[p]),
            hiddens[p],
            *blocks_of["hidden", p],
        )
        partials[p] = [mine] + [over_core(t) for t in theirs]

    def step_total(p):
        cuts = [2 if where in halved and rows % 32 == 0 else 1 for where in pieces[p]]
        results = ordered(lambda *a: add_blocks(cuts, *a), *partials[p])
        for (dy, dz), result in zip(pieces[p], results):
            if (dy, dz) in straight and (dy or dz):
                blocks_of["home", dy, dz] = [home(part, dy, dz) for part in result]
            elif dy:
                blocks_of["sum", dy, dz] = [over_y(part, -dy) for part in result]
            else:
                blocks_of["sum", dy, dz] = result

    def step_y(dz):
        wheres = [(dy, dz) for dy in range(ny) if (dy, dz) not in straight]
        parts = []
        for j in range(len(blocks_of["sum", *wheres[0]])):
            total = ordered(add, *[[blocks_of["sum", *where][j]] for where in wheres])
            parts.append(over_z(total, -dz))
        blocks_of["home", 0, dz] = parts

    F, Z, C, S = fetch_y, fetch_z, fetch_core, settle
    G, R, H, D, T, Y, L, W = (
        step_gate_up, step_send, step_hidden, step_down, step_total, step_y, step_load, step_early
    )
    blocks_of[0, 0] = [tokens]
    if ny == 2 and nz == 4 and cores == 2:
        pieces = [[(0, 0)], [(1, 0)], [(0, 1), (1, 1)], [(0, 2), (1, 2)], [(0, 3), (1, 3)]]
        straight = [(0, 1), (1, 1)]
        held, apart, spans = [0, 4], [1], [2, 2, 2, 2, 2]
        cut = []
        halved = [(0, 3), (1, 3)]
        plan = [
            (F, 1, 0), (Z, 1), (C, 0, 0), (G, 0), (R, 0), (S, (1, 0)), (C, 1, 0), (Z, 3), (C, 0, 1), (G, 1),
            (F, 1, 1), (Z, 2, 3), (F, 1, 2), (L,), (S, (1, 1)), (C, 1, 1), (H, 0), (G, 2), (H, 1), (C, 0, 3),
            (S, ("hidden", 1)), (S, ("hidden", 0)), (F, 1, 3), (S, ("hidden", 1)), (C, 1, 3), (D, 0), (D, 1),
            (C, 0, 2), (T, 0), (S, (1, 2)), (S, ("core", 0, 3)), (T, 1), (S, (0, 2)), (S, (1, 0)), (H, 2), (C, 1, 2),
            (G, 3), (S, ("sum", 1, 0)), (S, ("core", 1, 2)), (S, ("hidden", 0)), (D, 2), (G, 4), (R, 4), (T, 2),
            (H, 3), (D, 3), (S, ("home", 1, 1)), (S, (1, 2)), (T, 3), (H, 4), (Y, 2), (S, ("home", 0, 1)), (D, 4),
            (S, ("home", 1, 1)), (S, ("hidden", 3)), (S, (1, 2)), (S, ("home", 0, 2)), (T, 4), (Y, 3),
        ]
    else:
        pieces = [[(dy, dz)] for dz in [0] + others for dy in range(ny)]
        straight = []
        held, apart, cut, halved, spans = [], [], [], [], [1] * len(pieces)
        count = len(pieces)
        plan = [(F, dy, 0) for dy in range(1, ny)]
        for dz in others:
            plan += [(Z, dz)] + [(F, dy, dz) for dy in range(1, ny)]
        plan += [(C, *where) for piece in pieces for where in piece] + [(G, 0), (L,)]
        for p in range(count):
            plan += [(G, p + 1)] * (p + 1 < count) + [(H, p)] + [(D, p - 1), (T, p - 1)] * (p > 0)
        plan += [(D, count - 1), (T, count - 1)] + [(Y, dz) for dz in others]
    for step, *arguments in plan:
        step(*arguments)
    finals = [blocks_of["sum", dy, 0] for dy in range(ny)]
    finals += [value for key, value in blocks_of.items() if key[0] == "home"]
    return ordered(add, *finals)


def solution(mesh):
    sizes = dict(mesh.shape)
    return jax.shard_map(
        functools.partial(shards, sizes),
        mesh=mesh,
        in_specs=(
            P(("gx", "gy"), "gz"),
            P("gz", ("gx", "gy")),
            P("gz", ("gx", "gy")),
            P(("gx", "gy"), "gz"),
        ),
        out_specs=P(("gx", "gy"), "gz"),
        check_vma=False,
    )
```
